512 devices in a mesh: dp: 16 (over x, y_lo), tensor: 32 (over z, y_hi, core).
Axes of the slice: x: 4, y: 8 (y_hi: 2, y_lo: 4; y = y_hi * 4 + y_lo), z: 8, core: 2. Of those that a mesh axis runs over, the one named last changes fastest.
Arguments:
- grads: bfloat16 [16, 32, 16, 53248], P('dp', 'tensor'), may hold values from -6 to 6
- master: float32 [32, 16, 53248], P('tensor', 'dp'), may hold values from -6 to 6
- first_moment: float32 [32, 16, 53248], P('tensor', 'dp'), may hold values from -3 to 3
- second_moment: float32 [32, 16, 53248], P('tensor', 'dp'), may hold values from 0.01 to 1
Outputs:
- new_master: float32 [32, 16, 53248], P('tensor', 'dp')
- new_first: float32 [32, 16, 53248], P('tensor', 'dp')
- new_second: float32 [32, 16, 53248], P('tensor', 'dp')
- served: bfloat16 [512, 53248], P(None, 'tensor')
The draws below stay inside these ranges and needn't reach their ends.
All inputs are finite; a program needn't handle non-finite values.
Results may differ from the reference program's by a relative error of at most 0.0038.
Values may be sent and summed in bfloat16 or wider, within the bound.
A program may use at most 64 MiB of HBM per device.

```python
import math
import jax
import jax.numpy as jnp
from jax import lax

FF = 53248
SLAB_ROWS = 16
ROWS = 512
N_DP = 16
N_TENSOR = 32


def raised(values, stream_key, source, target, blocks, factor):
    owner, partner = [(jnp.arange(values.shape[dim]) // (values.shape[dim] // blocks)).reshape([-1 if axis == dim else 1 for axis in range(values.ndim)]) for dim in (source, target)]
    chosen = jax.random.permutation(stream_key, blocks)[partner]
    strong = (owner == chosen) | (owner == (partner + blocks // 2) % blocks)
    return jnp.where(strong, factor * values, values)


def steps_of(key, extent, split, least, top_value):
    level = 1.0
    for position, blocks in split:
        heights = jax.random.uniform(jax.random.fold_in(jax.random.fold_in(key, 6), position), (blocks,), jnp.float32, least / len(split), top_value / len(split))
        level = level * jnp.repeat(jnp.exp(heights), extent[position] // blocks).reshape((-1,) + (1,) * (len(extent) - 1 - position))
    return level


def bell_draw(key, dims, spread, limit, cuts=(), dtype=jnp.bfloat16):
    values = spread * jax.random.normal(key, dims, jnp.float32)
    if cuts:
        values = values * steps_of(key, dims, cuts, -0.22, 0.18)
    return jnp.clip(values, -limit, limit).astype(dtype)


def gaussian_with(own_key, shape, scale, bound, shards, heavy, kind=jnp.bfloat16):
    drawn = scale * jax.random.normal(own_key, shape, jnp.float32)
    if shards:
        drawn = drawn * steps_of(own_key, shape, shards, -0.22, 0.18)
    return jnp.clip(raised(drawn, jax.random.fold_in(own_key, 3), *heavy), -bound, bound).astype(kind)


def setup_inputs(seed: int = 0) -> dict:
    key_of = jax.random.split(jax.random.key(seed), 5)
    grads = gaussian_with(key_of[0], (N_DP, N_TENSOR, SLAB_ROWS, FF), 1.0, 6.0, ((0, 16), (1, 32)), (0, 2, 16, 2.0))
    master = bell_draw(key_of[1], (N_TENSOR, SLAB_ROWS, FF), 1.0, 6.0, ((0, 32), (1, 16)), jnp.float32)
    first_moment = bell_draw(key_of[2], (N_TENSOR, SLAB_ROWS, FF), 0.3, 3.0, ((0, 32), (1, 16)), jnp.float32)
    second_moment = jnp.clip(jnp.exp(math.log(1.0) - 4.6051702 * jax.random.uniform(key_of[3], (N_TENSOR, SLAB_ROWS, FF), jnp.float32) ** steps_of(key_of[3], (N_TENSOR, SLAB_ROWS, FF), ((0, 32), (1, 16)), -0.2, 0.2)), 0.01, 1.0)
    return {"grads": grads, "master": master, "first_moment": first_moment, "second_moment": second_moment}


def reference(grads, master, first_moment, second_moment):
    gradient = lax.optimization_barrier(jnp.sum(grads.astype(jnp.float32), axis=0)) / N_DP
    new_first = 0.9 * first_moment + 0.1 * gradient
    new_second = 0.95 * second_moment + 0.05 * gradient * gradient
    corr_first = 1.0 - 0.9 ** 10
    corr_second = 1.0 - 0.95 ** 10
    step_size = new_first / corr_first / (jnp.sqrt(new_second / corr_second) + 1e-08)
    new_master = master - 0.5 * (step_size + 0.1 * master)
    served = new_master.reshape(ROWS, FF).astype(jnp.bfloat16)
    return (new_master, new_first, new_second, served)
```

```python
import functools

import jax
import jax.numpy as jnp
from jax import lax
from jax.experimental import pallas as pl
from jax.experimental.pallas import tpu as pltpu
from jax.sharding import PartitionSpec as P

MESH = pl.DeviceIdType.MESH
F32, BF16 = jnp.float32, jnp.bfloat16
CHUNKS = (2, 3, 3, 3, 2)
FIRST = tuple(sum(CHUNKS[:k]) for k in range(len(CHUNKS)))
TILES = sum(CHUNKS)
STAGES = 5


def order():
    n = len(CHUNKS)
    return [
        (stage, step - stage)
        for step in range(n + STAGES)
        for stage in reversed(range(STAGES))
        if 0 <= step - stage < n
    ]


def kernel(
    g_hbm, m_hbm, f_hbm, s_hbm,
    om, of, os, served,
    gv, mv, fv, sv, perm, sendx, recvx, sendy, recvy, fresh, landed, mine, wide,
    load_sem, x_send, x_recv, y_send, y_recv, z_send, z_recv, z_own, w_send, w_recv, a_send, a_recv,
):
    dp, tn = lax.axis_index("dp"), lax.axis_index("tensor")
    x, yl = dp // 4, dp % 4
    z, yh, core = tn // 4, (tn // 2) % 2, tn % 2
    y = yh * 4 + yl
    q = core * 8 + z

    loads = [
        pltpu.make_async_copy(src, dst, load_sem.at[i])
        for i, (src, dst) in enumerate(((g_hbm, gv), (m_hbm, mv), (f_hbm, fv), (s_hbm, sv)))
    ]
    for copy in loads:
        copy.start()

    def device(dx=0, dy=0, dz=0, dc=0):
        to_y = (y + dy) % 8
        return ((x + dx) % 4) * 4 + to_y % 4, ((z + dz) % 8) * 4 + (to_y // 4) * 2 + (core + dc) % 2

    x_peers = [((x + d) % 4, device(dx=d)) for d in range(1, 4)]
    lo_peers = [((yl + d) % 4, (x * 4 + (yl + d) % 4, tn)) for d in range(1, 4)]
    y_peers = [(((y + d) % 8) // 4, device(dy=d)) for d in range(1, 8)]
    z_peers = [
        (((core + dc) % 2) * 8 + (z + dz) % 8, device(dz=dz, dc=dc))
        for dz in range(8) for dc in range(2) if (dz, dc) != (0, 0)
    ]

    barrier = pltpu.get_barrier_semaphore()
    greeted = x_peers + y_peers + z_peers
    for _, peer in greeted:
        pl.semaphore_signal(barrier, inc=1, device_id=peer, device_id_type=MESH)

    row = lax.broadcasted_iota(jnp.int32, (256, 256), 0)
    col = lax.broadcasted_iota(jnp.int32, (256, 256), 1)
    perm[...] = jnp.where(col == (row % 16) * 16 + row // 16, 1.0, 0.0).astype(BF16)

    def swap(rows):
        return jnp.dot(perm[...], rows, preferred_element_type=F32).astype(BF16)

    def remote(src, dst, send, recv, peer):
        return pltpu.make_async_remote_copy(
            src_ref=src, dst_ref=dst, send_sem=send, recv_sem=recv, device_id=peer, device_id_type=MESH
        )

    def tiles(k):
        return range(FIRST[k], FIRST[k] + CHUNKS[k])

    def span(k, per):
        return pl.ds(FIRST[k] * per, CHUNKS[k] * per)

    def x_copies(k):
        return [
            remote(sendx.at[to, :, span(k, 32)], recvx.at[d, :, span(k, 32)], x_send.at[k, d], x_recv.at[k, d], peer)
            for d, (to, peer) in enumerate(x_peers)
        ]

    def y_copies(k):
        return [
            remote(sendy.at[d, span(k, 32)], recvy.at[d, span(k, 32)], y_send.at[k, d], y_recv.at[k, d], peer)
            for d, (_, peer) in enumerate(lo_peers)
        ]

    def z_copies(k):
        return [
            remote(fresh.at[span(k, 1), :, to], landed.at[span(k, 1), :, q], z_send.at[k, d], z_recv.at[k, d], peer)
            for d, (to, peer) in enumerate(z_peers)
        ]

    def z_local(k):
        return pltpu.make_async_copy(fresh.at[span(k, 1), :, q], landed.at[span(k, 1), :, q], z_own.at[k])

    def w_copies(k):
        return [
            remote(mine.at[to, span(k, 16)], wide.at[x, yl, yh, span(k, 16)], w_send.at[k, d], w_recv.at[k, d], peer)
            for d, (to, peer) in enumerate(y_peers)
        ]

    def a_copies(k):
        return [
            remote(wide.at[x, :, :, span(k, 16)], wide.at[x, :, :, span(k, 16)], a_send.at[k, d], a_recv.at[k, d], peer)
            for d, (_, peer) in enumerate(x_peers)
        ]

    def split(k):
        for c in tiles(k):
            halves = []
            for h in range(2):
                columns = [((i % 8 * 4 + h * 2 + i // 8) * TILES + c) * 128 for i in range(16)]
                halves.append(jnp.concatenate([gv[:, at : at + 128] for at in columns], axis=0))
            out = swap(jnp.concatenate(halves, axis=1))
            for j in range(16):
                for h in range(2):
                    sendx[j // 4, j % 4, c * 32 + h * 16 : c * 32 + h * 16 + 16, :] = (
                        out[j * 16 : j * 16 + 16, h * 128 : h * 128 + 128]
                    )

    def over_x(to, rows):
        total = sendx[x, to, rows, :].astype(F32)
        for d in range(3):
            total += recvx[d, to, rows, :].astype(F32)
        return total

    def reduce_x(k):
        for copy in x_copies(k):
            copy.wait_recv()
        for d, (to, _) in enumerate(lo_peers):
            sendy[d, span(k, 32), :] = over_x(to, span(k, 32)).astype(BF16)
        for copy in y_copies(k):
            copy.start()

    def update(k):
        if k == 0:
            for copy in loads[1:]:
                copy.wait()
        for copy in y_copies(k):
            copy.wait_recv()
        for c in tiles(k):
            for h in range(2):
                rows = pl.ds(c * 32 + h * 16, 16)
                total = over_x(yl, rows)
                for d in range(3):
                    total += recvy[d, rows, :].astype(F32)
                total = total / 16
                for e in range(2):
                    gradient = total[e * 8 : e * 8 + 8]
                    at = pl.ds(h * 2 * TILES + e * TILES + c, 8, stride=4 * TILES)
                    first = 0.9 * fv[at, :] + 0.1 * gradient
                    second = 0.95 * sv[at, :] + 0.05 * gradient * gradient
                    of[at, :] = first
                    os[at, :] = second
                    step = first / (1.0 - 0.9**10) / (jnp.sqrt(second / (1.0 - 0.95**10)) + 1e-08)
                    old = mv[at, :]
                    new = old - 0.5 * (step + 0.1 * old)
                    om[at, :] = new
                    for i in range(8):
                        fresh[c, h, e * 8 + i, :, :] = new[i : i + 1]
        z_local(k).start()
        for copy in z_copies(k):
            copy.start()

    def spread(k):
        z_local(k).wait()
        for copy in z_copies(k):
            copy.wait_recv()
        for c in tiles(k):
            for h in range(2):
                block = jnp.concatenate([landed[c, h, i, :, :] for i in range(16)], axis=0).astype(BF16)
                mine[h, c * 16 : c * 16 + 16, :] = block
        for copy in w_copies(k):
            copy.start()
        wide[x, yl, yh, span(k, 16), :] = mine[yh, span(k, 16), :]

    def gather(k):
        for copy in w_copies(k):
            copy.wait_recv()
        for copy in a_copies(k):
            copy.start()

    def serve(k):
        for copy in a_copies(k):
            copy.wait_recv()
        for c in tiles(k):
            halves = [
                jnp.concatenate([wide[j // 4, j % 4, h, c * 16 : c * 16 + 16, :] for j in range(16)], axis=0)
                for h in range(2)
            ]
            out = swap(jnp.concatenate(halves, axis=1))
            for i in range(16):
                for h in range(2):
                    t = i % 8 * 4 + h * 2 + i // 8
                    served[t * 16 : t * 16 + 16, c * 128 : c * 128 + 128] = (
                        out[i * 16 : i * 16 + 16, h * 128 : h * 128 + 128]
                    )

    loads[0].wait()
    split(0)
    pl.semaphore_wait(barrier, len(greeted))
    for copy in x_copies(0):
        copy.start()
    for k in range(1, len(CHUNKS)):
        split(k)
        for copy in x_copies(k):
            copy.start()
    for stage, k in order():
        (reduce_x, update, spread, gather, serve)[stage](k)
    for k in range(len(CHUNKS)):
        for copies in (x_copies, y_copies, z_copies, w_copies, a_copies):
            for copy in copies(k):
                copy.wait_send()


def local(grads, master, first_moment, second_moment):
    n = len(CHUNKS)
    rows = TILES * 32
    dma = pltpu.SemaphoreType.DMA
    vmem = pltpu.VMEM
    flat = jax.ShapeDtypeStruct((rows, 128), F32)
    outs = pl.pallas_call(
        kernel,
        name="refit",
        out_shape=(flat, flat, flat, jax.ShapeDtypeStruct((512, TILES * 128), BF16)),
        in_specs=[pl.BlockSpec(memory_space=pltpu.HBM)] * 4,
        out_specs=[pl.BlockSpec(memory_space=vmem)] * 4,
        scratch_shapes=[
            vmem((16, rows * 128), BF16),
            vmem((rows, 128), F32),
            vmem((rows, 128), F32),
            vmem((rows, 128), F32),
            vmem((256, 256), BF16),
            vmem((4, 4, rows, 128), BF16),
            vmem((3, 4, rows, 128), BF16),
            vmem((3, rows, 128), BF16),
            vmem((3, rows, 128), BF16),
            vmem((TILES, 2, 16, 1, 128), F32),
            vmem((TILES, 2, 16, 1, 128), F32),
            vmem((2, TILES * 16, 128), BF16),
            vmem((4, 4, 2, TILES * 16, 128), BF16),
            dma((4,)),
            dma((n, 3)), dma((n, 3)),
            dma((n, 3)), dma((n, 3)),
            dma((n, 15)), dma((n, 15)), dma((n,)),
            dma((n, 7)), dma((n, 7)),
            dma((n, 3)), dma((n, 3)),
        ],
        compiler_params=pltpu.CompilerParams(
            collective_id=0, has_side_effects=True, vmem_limit_bytes=60 * 2**20
        ),
    )(
        grads.reshape(16, rows * 128),
        master.reshape(rows, 128),
        first_moment.reshape(rows, 128),
        second_moment.reshape(rows, 128),
    )
    new_master, new_first, new_second, served = outs
    shape = master.shape
    return new_master.reshape(shape), new_first.reshape(shape), new_second.reshape(shape), served


def solution(mesh):
    in_specs = (
        P("dp", "tensor", None, None),
        P("tensor", "dp", None),
        P("tensor", "dp", None),
        P("tensor", "dp", None),
    )
    out_specs = (
        P("tensor", "dp", None),
        P("tensor", "dp", None),
        P("tensor", "dp", None),
        P(None, "tensor"),
    )
    return jax.shard_map(local, mesh=mesh, in_specs=in_specs, out_specs=out_specs, check_vma=False)
```

```python
import functools

import jax
import jax.numpy as jnp
from jax import lax
from jax.experimental import pallas as pl
from jax.experimental.pallas import tpu as pltpu
from jax.sharding import PartitionSpec as P

MESH = pl.DeviceIdType.MESH
F32, BF16 = jnp.float32, jnp.bfloat16
CHUNKS = (1, 3, 3, 3, 2, 1)
FIRST = tuple(sum(CHUNKS[:k]) for k in range(len(CHUNKS)))
TILES = sum(CHUNKS)
TILE_US = 1.4
HOPS_US = (2.9, 3.5, 5.7, 5.2, 2.9)


def order():
    ready, link, gathers = [], 0.0, 0.0
    for k, tiles in enumerate(CHUNKS):
        link += tiles * TILE_US
        at = link + HOPS_US[0]
        for stage in range(4):
            ready.append((at, stage, k))
            at += HOPS_US[stage + 1] if stage < 3 else 0.0
        gathers = max(at, gathers) + tiles * TILE_US
        ready.append((gathers + HOPS_US[4], 4, k))
    return [(stage, k) for _, stage, k in sorted(ready)]


def kernel(
    g_hbm, m_hbm, f_hbm, s_hbm,
    om, of, os, served,
    gv, mv, fv, sv, perm, sendx, recvx, sendy, recvy, fresh, landed, mine, wide,
    load_sem, x_send, y_send, z_send, w_send, a_send, x_recv, y_recv, z_recv, w_recv, a_recv,
):
    dp, tn = lax.axis_index("dp"), lax.axis_index("tensor")
    x, yl = dp // 4, dp % 4
    z, yh, core = tn // 4, (tn // 2) % 2, tn % 2
    y = yh * 4 + yl
    q = core * 8 + z

    quarter = TILES * 1024
    loads = [
        pltpu.make_async_copy(g_hbm.at[:, i : i + quarter], gv.at[:, i : i + quarter], load_sem.at[0])
        for i in range(0, 4 * quarter, quarter)
    ]
    loads += [
        pltpu.make_async_copy(src, dst, load_sem.at[1 + i])
        for i, (src, dst) in enumerate(((m_hbm, mv), (f_hbm, fv), (s_hbm, sv)))
    ]
    for copy in loads:
        copy.start()

    def device(dx=0, dy=0, dz=0, dc=0):
        to_y = (y + dy) % 8
        return ((x + dx) % 4) * 4 + to_y % 4, ((z + dz) % 8) * 4 + (to_y // 4) * 2 + (core + dc) % 2

    x_peers = [((x + d) % 4, device(dx=d)) for d in range(1, 4)]
    lo_peers = [((yl + d) % 4, (x * 4 + (yl + d) % 4, tn)) for d in range(1, 4)]
    y_peers = [(((y + d) % 8) // 4, device(dy=d)) for d in range(1, 8)]
    z_peers = [
        (((core + dc) % 2) * 8 + (z + dz) % 8, device(dz=dz, dc=dc))
        for dz in range(8) for dc in range(2) if (dz, dc) != (0, 0)
    ]

    barrier = pltpu.get_barrier_semaphore()
    greeted = x_peers + y_peers + z_peers
    for _, peer in greeted:
        pl.semaphore_signal(barrier, inc=1, device_id=peer, device_id_type=MESH)

    row = lax.broadcasted_iota(jnp.int32, (256, 256), 0)
    col = lax.broadcasted_iota(jnp.int32, (256, 256), 1)
    perm[...] = jnp.where(col == (row % 16) * 16 + row // 16, 1.0, 0.0).astype(BF16)

    def swap(rows):
        return jnp.dot(perm[...], rows, preferred_element_type=F32).astype(BF16)

    def remote(src, dst, send, recv, peer):
        return pltpu.make_async_remote_copy(
            src_ref=src, dst_ref=dst, send_sem=send, recv_sem=recv, device_id=peer, device_id_type=MESH
        )

    def tiles(k):
        return range(FIRST[k], FIRST[k] + CHUNKS[k])

    def span(k, per):
        return pl.ds(FIRST[k] * per, CHUNKS[k] * per)

    def x_copies(k):
        return [
            remote(sendx.at[to, :, span(k, 32)], recvx.at[d, :, span(k, 32)], x_send, x_recv.at[k], peer)
            for d, (to, peer) in enumerate(x_peers)
        ]

    def y_copies(k):
        return [
            remote(sendy.at[d, span(k, 32)], recvy.at[d, span(k, 32)], y_send, y_recv.at[k], peer)
            for d, (_, peer) in enumerate(lo_peers)
        ]

    def z_copies(k):
        own = pltpu.make_async_copy(fresh.at[span(k, 1), :, q], landed.at[span(k, 1), :, q], z_recv.at[k])
        return [own] + [
            remote(fresh.at[span(k, 1), :, to], landed.at[span(k, 1), :, q], z_send, z_recv.at[k], peer)
            for to, peer in z_peers
        ]

    def w_copies(k):
        return [
            remote(mine.at[to, span(k, 16)], wide.at[dp, yh, span(k, 16)], w_send, w_recv.at[k], peer)
            for to, peer in y_peers
        ]

    def a_copies(k):
        own = wide.at[pl.ds(x * 4, 4), :, span(k, 16)]
        return [remote(own, own, a_send, a_recv.at[k], peer) for _, peer in x_peers]

    def wait(ref, sem):
        pltpu.make_async_copy(ref, ref, sem).wait()

    def split(k):
        for c in tiles(k):
            halves = []
            for h in range(2):
                columns = [((i % 8 * 4 + h * 2 + i // 8) * TILES + c) * 128 for i in range(16)]
                halves.append(jnp.concatenate([gv[:, at : at + 128] for at in columns], axis=0))
            out = swap(jnp.concatenate(halves, axis=1))
            for j in range(16):
                for h in range(2):
                    sendx[j // 4, j % 4, c * 32 + h * 16 : c * 32 + h * 16 + 16, :] = (
                        out[j * 16 : j * 16 + 16, h * 128 : h * 128 + 128]
                    )

    def over_x(to, rows):
        total = sendx[x, to, rows, :].astype(F32)
        for d in range(3):
            total += recvx[d, to, rows, :].astype(F32)
        return total

    def reduce_x(k):
        wait(recvx.at[:, :, span(k, 32)], x_recv.at[k])
        for d, (to, _) in enumerate(lo_peers):
            sendy[d, span(k, 32), :] = over_x(to, span(k, 32)).astype(BF16)
        for copy in y_copies(k):
            copy.start()

    def update(k):
        if k == 0:
            for copy in loads[4:]:
                copy.wait()
        wait(recvy.at[:, span(k, 32)], y_recv.at[k])
        for c in tiles(k):
            for h in range(2):
                rows = pl.ds(c * 32 + h * 16, 16)
                total = over_x(yl, rows)
                for d in range(3):
                    total += recvy[d, rows, :].astype(F32)
                total = total / 16
                for e in range(2):
                    gradient = total[e * 8 : e * 8 + 8]
                    at = pl.ds(h * 2 * TILES + e * TILES + c, 8, stride=4 * TILES)
                    first = 0.9 * fv[at, :] + 0.1 * gradient
                    second = 0.95 * sv[at, :] + 0.05 * gradient * gradient
                    of[at, :] = first
                    os[at, :] = second
                    step = first / (1.0 - 0.9**10) / (jnp.sqrt(second / (1.0 - 0.95**10)) + 1e-08)
                    old = mv[at, :]
                    new = old - 0.5 * (step + 0.1 * old)
                    om[at, :] = new
                    for i in range(8):
                        fresh[c, h, e * 8 + i, :, :] = new[i : i + 1]
        for copy in z_copies(k):
            copy.start()

    def spread(k):
        wait(landed.at[span(k, 1)], z_recv.at[k])
        for c in tiles(k):
            for h in range(2):
                block = jnp.concatenate([landed[c, h, i, :, :] for i in range(16)], axis=0).astype(BF16)
                mine[h, c * 16 : c * 16 + 16, :] = block
        for copy in w_copies(k):
            copy.start()
        wide[dp, yh, span(k, 16), :] = mine[yh, span(k, 16), :]

    def gather(k):
        wait(wide.at[0:7, 0, span(k, 16)], w_recv.at[k])
        for copy in a_copies(k):
            copy.start()

    def serve(k):
        wait(wide.at[0:12, :, span(k, 16)], a_recv.at[k])
        for c in tiles(k):
            halves = [
                jnp.concatenate([wide[j, h, c * 16 : c * 16 + 16, :] for j in range(16)], axis=0)
                for h in range(2)
            ]
            out = swap(jnp.concatenate(halves, axis=1))
            for i in range(16):
                for h in range(2):
                    t = i % 8 * 4 + h * 2 + i // 8
                    served[t * 16 : t * 16 + 16, c * 128 : c * 128 + 128] = (
                        out[i * 16 : i * 16 + 16, h * 128 : h * 128 + 128]
                    )

    wait(gv, load_sem.at[0])
    split(0)
    pl.semaphore_wait(barrier, len(greeted))
    for copy in x_copies(0):
        copy.start()
    for k in range(1, len(CHUNKS)):
        split(k)
        for copy in x_copies(k):
            copy.start()
    for stage, k in order():
        (reduce_x, update, spread, gather, serve)[stage](k)
    for ref, sem in (
        (recvx, x_send),
        (recvy, y_send),
        (landed.at[:, :, 0:15], z_send),
        (wide.at[0:7, 0], w_send),
        (wide.at[0:12], a_send),
    ):
        wait(ref, sem)


def store(*refs):
    copies = [pltpu.make_async_copy(refs[i], refs[4 + i], refs[8].at[i]) for i in (3, 0, 1, 2)]
    for copy in copies:
        copy.start()
    for copy in copies:
        copy.wait()


def local(grads, master, first_moment, second_moment):
    n = len(CHUNKS)
    rows = TILES * 32
    dma = pltpu.SemaphoreType.DMA
    vmem = pltpu.VMEM
    shapes = ((rows, 128), F32), ((rows, 128), F32), ((rows, 128), F32), ((512, TILES * 128), BF16)
    outs = pl.pallas_call(
        kernel,
        name="refit",
        out_shape=[vmem(*shape) for shape in shapes],
        in_specs=[pl.BlockSpec(memory_space=pltpu.HBM)] * 4,
        out_specs=[pl.BlockSpec(memory_space=vmem)] * 4,
        scratch_shapes=[
            vmem((16, rows * 128), BF16),
            vmem((rows, 128), F32),
            vmem((rows, 128), F32),
            vmem((rows, 128), F32),
            vmem((256, 256), BF16),
            vmem((4, 4, rows, 128), BF16),
            vmem((3, 4, rows, 128), BF16),
            vmem((3, rows, 128), BF16),
            vmem((3, rows, 128), BF16),
            vmem((TILES, 2, 16, 1, 128), F32),
            vmem((TILES, 2, 16, 1, 128), F32),
            vmem((2, TILES * 16, 128), BF16),
            vmem((16, 2, TILES * 16, 128), BF16),
            dma((4,)),
            *([dma] * 5),
            *([dma((n,))] * 5),
        ],
        compiler_params=pltpu.CompilerParams(
            collective_id=0, has_side_effects=True, vmem_limit_bytes=60 * 2**20
        ),
    )(
        *(
            pltpu.with_memory_space_constraint(v, pltpu.HBM)
            for v in (
                grads.reshape(16, rows * 128),
                master.reshape(rows, 128),
                first_moment.reshape(rows, 128),
                second_moment.reshape(rows, 128),
            )
        )
    )
    outs = pl.pallas_call(
        store,
        name="store",
        out_shape=[jax.ShapeDtypeStruct(*shape) for shape in shapes],
        in_specs=[pl.BlockSpec(memory_space=vmem)] * 4,
        out_specs=[pl.BlockSpec(memory_space=pltpu.HBM)] * 4,
        scratch_shapes=[dma((4,))],
        compiler_params=pltpu.CompilerParams(vmem_limit_bytes=2**20),
    )(*outs)
    new_master, new_first, new_second, served = outs
    shape = master.shape
    return new_master.reshape(shape), new_first.reshape(shape), new_second.reshape(shape), served


def solution(mesh):
    in_specs = (
        P("dp", "tensor", None, None),
        P("tensor", "dp", None),
        P("tensor", "dp", None),
        P("tensor", "dp", None),
    )
    out_specs = (
        P("tensor", "dp", None),
        P("tensor", "dp", None),
        P("tensor", "dp", None),
        P(None, "tensor"),
    )
    return jax.shard_map(local, mesh=mesh, in_specs=in_specs, out_specs=out_specs, check_vma=False)
```

```python
import jax
import jax.numpy as jnp
from jax import lax
from jax.experimental import pallas as pl
from jax.experimental.pallas import tpu as pltpu
from jax.sharding import PartitionSpec as P

MESH = pl.DeviceIdType.MESH
F32, BF16 = jnp.float32, jnp.bfloat16
CHUNKS = (1, 2, 2, 2, 2, 2, 2)
DOWN = "BRRABAA"
UP = "ARRRRBA"
FIRST = tuple(sum(CHUNKS[:k]) for k in range(len(CHUNKS)))
TILES = sum(CHUNKS)
ORDER = (
    ("send", 1), ("bsend", 0), ("bsend", 4), ("send", 2), ("send", 3), ("relay", 1), ("bred", 0),
    ("relay", 2), ("send", 5), ("redx", 3), ("redx", 1), ("upd", 0), ("send", 6), ("redx", 2),
    ("bred", 4), ("upd", 3), ("redx", 5), ("upd", 1), ("spread", 0), ("upd", 2), ("redx", 6),
    ("upd", 4), ("upd", 5), ("spread", 3), ("spread", 1), ("upd", 6), ("gath", 0), ("spread", 2),
    ("spread", 4), ("bspread", 5), ("gath", 3), ("serve", 0), ("gath", 1), ("spread", 6),
    ("bgath", 5), ("gath", 2), ("fwd", 3), ("gath", 4), ("fwd", 1), ("fwd", 2), ("gath", 6),
    ("serve", 3), ("fwd", 4), ("serve", 1), ("serve", 2), ("serve", 5), ("serve", 6), ("serve", 4),
)


def kernel(
    g_hbm, m_hbm, f_hbm, s_hbm,
    om, of, os, served,
    gv, mv, fv, sv, perm, parts, got, passed, sums, got_sums, fresh, landed, mine, crossed, wide,
    load_sem, x_send, y_send, z_send, w_send, a_send, x_recv, y_recv, z_recv, w_recv, a_recv, p_recv, f_recv,
):
    dp, tn = lax.axis_index("dp"), lax.axis_index("tensor")
    x, yl = dp // 4, dp % 4
    z, yh, core = tn // 4, (tn // 2) % 2, tn % 2
    y = yh * 4 + yl
    q = core * 8 + z
    right, left, across = (x + 1) % 4, (x + 3) % 4, (x + 2) % 4

    def device(dx=0, dy=0, dz=0, dc=0):
        to_y = (y + dy) % 8
        return ((x + dx) % 4) * 4 + to_y % 4, ((z + dz) % 8) * 4 + (to_y // 4) * 2 + (core + dc) % 2

    to_right, to_left = device(dx=1), device(dx=3)
    x_peers = [((x + d) % 4, device(dx=d)) for d in (2, 1, 3)]
    lo_peers = [((yl + d) % 4, (x * 4 + (yl + d) % 4, tn)) for d in range(1, 4)]
    y_peers = [(((y + d) % 8) // 4, device(dy=d)) for d in (4, 3, 5, 2, 6, 1, 7)]
    z_peers = [
        (((core + dc) % 2) * 8 + (z + dz) % 8, device(dz=dz, dc=dc))
        for dz in (4, 3, 5, 2, 6, 1, 7, 0) for dc in (1, 0) if (dz, dc) != (0, 0)
    ]

    barrier = pltpu.get_barrier_semaphore()
    greeted = x_peers + y_peers + z_peers
    for _, peer in greeted:
        pl.semaphore_signal(barrier, inc=1, device_id=peer, device_id_type=MESH)

    k0 = ORDER[0][1]
    lo, hi = FIRST[k0] * 128, (FIRST[k0] + CHUNKS[k0]) * 128
    width = TILES * 128

    def fetch(first, last, sem):
        for i in range(0, 32 * width, width):
            cut = pl.ds(i + first, last - first)
            pltpu.make_async_copy(g_hbm.at[:, cut], gv.at[:, cut], sem).start()

    fetch(lo, hi, load_sem.at[0])
    if lo:
        fetch(0, lo, load_sem.at[4])
    fetch(hi, width, load_sem.at[4])
    loads = [
        pltpu.make_async_copy(src, dst, load_sem.at[1 + i])
        for i, (src, dst) in enumerate(((m_hbm, mv), (f_hbm, fv), (s_hbm, sv)))
    ]
    for copy in loads:
        copy.start()

    row = lax.broadcasted_iota(jnp.int32, (256, 256), 0)
    col = lax.broadcasted_iota(jnp.int32, (256, 256), 1)
    perm[...] = jnp.where(col == (row % 16) * 16 + row // 16, 1.0, 0.0).astype(BF16)

    def swap(rows):
        return jnp.dot(perm[...], rows, preferred_element_type=F32).astype(BF16)

    def wait(tiles, sem):
        ref = gv.at[:, 0 : tiles * 128]
        pltpu.make_async_copy(ref, ref, sem).wait()

    def remote(src, dst, send, recv, peer):
        pltpu.make_async_remote_copy(
            src_ref=src, dst_ref=dst, send_sem=send, recv_sem=recv, device_id=peer, device_id_type=MESH
        ).start()

    def tiles(k):
        return range(FIRST[k], FIRST[k] + CHUNKS[k])

    def span(k, per):
        return pl.ds(FIRST[k] * per, CHUNKS[k] * per)

    def split(k):
        for c in tiles(k):
            halves = []
            for h in range(2):
                columns = [((i % 8 * 4 + h * 2 + i // 8) * TILES + c) * 128 for i in range(16)]
                halves.append(jnp.concatenate([gv[:, at : at + 128] for at in columns], axis=0))
            out = swap(jnp.concatenate(halves, axis=1))
            for j in range(16):
                for h in range(2):
                    parts[j // 4, j % 4, c * 32 + h * 16 : c * 32 + h * 16 + 16, :] = (
                        out[j * 16 : j * 16 + 16, h * 128 : h * 128 + 128]
                    )

    def send(k):
        split(k)
        if (send.__name__, k) == ORDER[0]:
            pl.semaphore_wait(barrier, len(greeted))
        at = span(k, 32)
        if DOWN[k] == "R":
            remote(parts.at[across, 0:2, at], passed.at[0, :, at], x_send, p_recv.at[k], to_right)
            remote(parts.at[across, 2:4, at], passed.at[1, :, at], x_send, p_recv.at[k], to_left)
            remote(parts.at[right, 2:4, at], got.at[0, 2:4, at], x_send, x_recv.at[k], to_right)
            remote(parts.at[left, 0:2, at], got.at[1, 0:2, at], x_send, x_recv.at[k], to_left)
        else:
            for d, (to, peer) in enumerate(x_peers):
                remote(parts.at[to, :, at], got.at[d, :, at], x_send, x_recv.at[k], peer)

    def relay(k):
        wait(CHUNKS[k] * 8, p_recv.at[k])
        at = span(k, 32)
        for way, (to, first, peer) in enumerate(((right, 0, to_right), (left, 2, to_left))):
            for i in range(2):
                passed[way, i, at, :] = (
                    passed[way, i, at, :].astype(F32) + parts[to, first + i, at, :].astype(F32)
                ).astype(BF16)
            remote(passed.at[way, :, at], got.at[way, first : first + 2, at], x_send, x_recv.at[k], peer)

    def received(k):
        return 2 if DOWN[k] == "R" else 3

    def redx(k):
        wait(CHUNKS[k] * 8 * received(k), x_recv.at[k])
        at = span(k, 32)
        for d, (to, peer) in enumerate(lo_peers):
            total = parts[x, to, at, :].astype(F32)
            for i in range(received(k)):
                total += got[i, to, at, :].astype(F32)
            sums[d, at, :] = total.astype(BF16)
            remote(sums.at[d, at], got_sums.at[d, at], y_send, y_recv.at[k], peer)

    def bsend(k):
        split(k)
        at = span(k, 32)
        for d, (to, peer) in enumerate(lo_peers):
            remote(parts.at[:, to, at], got.at[d, :, at], x_send, x_recv.at[k], peer)

    def bred(k):
        wait(CHUNKS[k] * 24, x_recv.at[k])
        at = span(k, 32)
        for d, (to, peer) in enumerate(x_peers):
            total = parts[to, yl, at, :].astype(F32)
            for i in range(3):
                total += got[i, to, at, :].astype(F32)
            sums[d, at, :] = total.astype(BF16)
            remote(sums.at[d, at], got_sums.at[d, at], y_send, y_recv.at[k], peer)

    def upd(k):
        wait(CHUNKS[k] * 6, y_recv.at[k])
        own = x if DOWN[k] == "B" else yl
        for c in tiles(k):
            for h in range(2):
                rows = pl.ds(c * 32 + h * 16, 16)
                total = parts[x, yl, rows, :].astype(F32)
                for i in range(received(k)):
                    total += got[i, own, rows, :].astype(F32)
                for i in range(3):
                    total += got_sums[i, rows, :].astype(F32)
                total = total / 16
                for e in range(2):
                    gradient = total[e * 8 : e * 8 + 8]
                    at = pl.ds(h * 2 * TILES + e * TILES + c, 8, stride=4 * TILES)
                    first = 0.9 * fv[at, :] + 0.1 * gradient
                    second = 0.95 * sv[at, :] + 0.05 * gradient * gradient
                    of[at, :] = first
                    os[at, :] = second
                    step = first / (1.0 - 0.9**10) / (jnp.sqrt(second / (1.0 - 0.95**10)) + 1e-08)
                    old = mv[at, :]
                    new = old - 0.5 * (step + 0.1 * old)
                    om[at, :] = new
                    for i in range(8):
                        fresh[c, h, e * 8 + i, :, :] = new[i : i + 1]
        at = span(k, 1)
        for to, peer in z_peers:
            remote(fresh.at[at, :, to], landed.at[at, :, q], z_send, z_recv.at[k], peer)
        pltpu.make_async_copy(fresh.at[at, :, q], landed.at[at, :, q], z_recv.at[k]).start()

    def collect(k):
        wait(CHUNKS[k] * 4, z_recv.at[k])
        for c in tiles(k):
            for h in range(2):
                block = jnp.concatenate([landed[c, h, i, :, :] for i in range(16)], axis=0)
                mine[h, c * 16 : c * 16 + 16, :] = block.astype(BF16)

    def spread(k):
        collect(k)
        at = span(k, 16)
        for to, peer in y_peers:
            remote(mine.at[to, at], wide.at[x, yl, yh, at], w_send, w_recv.at[k], peer)
        pltpu.make_async_copy(mine.at[yh, at], wide.at[x, yl, yh, at], w_recv.at[k]).start()

    def gath(k):
        wait(CHUNKS[k] * 8, w_recv.at[k])
        own = wide.at[x, :, :, span(k, 16)]
        for peer in (to_right, to_left) if UP[k] == "R" else [peer for _, peer in x_peers]:
            remote(own, own, a_send, a_recv.at[k], peer)

    def fwd(k):
        wait(CHUNKS[k] * 16, a_recv.at[k])
        for source, first, peer in ((left, 0, to_right), (right, 2, to_left)):
            block = wide.at[source, first : first + 2, :, span(k, 16)]
            remote(block, block, a_send, f_recv.at[k], peer)

    def bspread(k):
        collect(k)
        at = span(k, 16)
        for _, peer in x_peers:
            remote(mine.at[:, at], crossed.at[x, :, at], w_send, w_recv.at[k], peer)
        pltpu.make_async_copy(mine.at[:, at], crossed.at[x, :, at], w_recv.at[k]).start()

    def bgath(k):
        wait(CHUNKS[k] * 8, w_recv.at[k])
        at = span(k, 16)
        for to, peer in y_peers:
            remote(crossed.at[:, to, at], wide.at[:, yl, yh, at], a_send, a_recv.at[k], peer)
        pltpu.make_async_copy(crossed.at[:, yh, at], wide.at[:, yl, yh, at], a_recv.at[k]).start()

    def serve(k):
        if UP[k] == "R":
            wait(CHUNKS[k] * 8, f_recv.at[k])
        else:
            wait(CHUNKS[k] * (32 if UP[k] == "B" else 24), a_recv.at[k])
        for c in tiles(k):
            halves = [
                jnp.concatenate([wide[j // 4, j % 4, h, c * 16 : c * 16 + 16, :] for j in range(16)], axis=0)
                for h in range(2)
            ]
            out = swap(jnp.concatenate(halves, axis=1))
            for i in range(16):
                for h in range(2):
                    t = i % 8 * 4 + h * 2 + i // 8
                    served[t * 16 : t * 16 + 16, c * 128 : c * 128 + 128] = (
                        out[i * 16 : i * 16 + 16, h * 128 : h * 128 + 128]
                    )

    stages = {
        f.__name__: f for f in (send, relay, redx, bsend, bred, upd, spread, gath, fwd, bspread, bgath, serve)
    }
    wait(CHUNKS[k0] * 32, load_sem.at[0])
    for i, (stage, k) in enumerate(ORDER):
        if i == 1:
            wait((TILES - CHUNKS[k0]) * 32, load_sem.at[4])
        if stage == "upd" and "upd" not in [name for name, _ in ORDER[:i]]:
            for copy in loads:
                copy.wait()
        stages[stage](k)

    crosswise = sum(c for c, kind in zip(CHUNKS, UP) if kind == "B")
    straight = TILES - crosswise
    wait(TILES * 24, x_send)
    wait(TILES * 6, y_send)
    sent = landed.at[:, :, 0:15]
    pltpu.make_async_copy(sent, sent, z_send).wait()
    wait(straight * 7 + crosswise * 6, w_send)
    wait(straight * 24 + crosswise * 28, a_send)


def store(*refs):
    copies = [pltpu.make_async_copy(refs[i], refs[4 + i], refs[8].at[i]) for i in (3, 0, 1, 2)]
    for copy in copies:
        copy.start()
    for copy in copies:
        copy.wait()


def local(grads, master, first_moment, second_moment):
    n = len(CHUNKS)
    rows = TILES * 32
    dma = pltpu.SemaphoreType.DMA
    vmem = pltpu.VMEM
    shapes = ((rows, 128), F32), ((rows, 128), F32), ((rows, 128), F32), ((512, TILES * 128), BF16)
    outs = pl.pallas_call(
        kernel,
        name="refit",
        out_shape=[vmem(*shape) for shape in shapes],
        in_specs=[pl.BlockSpec(memory_space=pltpu.HBM)] * 4,
        out_specs=[pl.BlockSpec(memory_space=vmem)] * 4,
        scratch_shapes=[
            vmem((16, rows * 128), BF16),
            vmem((rows, 128), F32),
            vmem((rows, 128), F32),
            vmem((rows, 128), F32),
            vmem((256, 256), BF16),
            vmem((4, 4, rows, 128), BF16),
            vmem((3, 4, rows, 128), BF16),
            vmem((2, 2, rows, 128), BF16),
            vmem((3, rows, 128), BF16),
            vmem((3, rows, 128), BF16),
            vmem((TILES, 2, 16, 1, 128), F32),
            vmem((TILES, 2, 16, 1, 128), F32),
            vmem((2, TILES * 16, 128), BF16),
            vmem((4, 2, TILES * 16, 128), BF16),
            vmem((4, 4, 2, TILES * 16, 128), BF16),
            dma((5,)),
            *([dma] * 5),
            *([dma((n,))] * 7),
        ],
        compiler_params=pltpu.CompilerParams(
            collective_id=0, has_side_effects=True, vmem_limit_bytes=60 * 2**20
        ),
    )(
        *(
            pltpu.with_memory_space_constraint(v, pltpu.HBM)
            for v in (
                grads.reshape(16, rows * 128),
                master.reshape(rows, 128),
                first_moment.reshape(rows, 128),
                second_moment.reshape(rows, 128),
            )
        )
    )
    outs = pl.pallas_call(
        store,
        name="store",
        out_shape=[jax.ShapeDtypeStruct(*shape) for shape in shapes],
        in_specs=[pl.BlockSpec(memory_space=vmem)] * 4,
        out_specs=[pl.BlockSpec(memory_space=pltpu.HBM)] * 4,
        scratch_shapes=[dma((4,))],
        compiler_params=pltpu.CompilerParams(vmem_limit_bytes=2**20),
    )(*outs)
    new_master, new_first, new_second, served = outs
    shape = master.shape
    return new_master.reshape(shape), new_first.reshape(shape), new_second.reshape(shape), served


def solution(mesh):
    in_specs = (
        P("dp", "tensor", None, None),
        P("tensor", "dp", None),
        P("tensor", "dp", None),
        P("tensor", "dp", None),
    )
    out_specs = (
        P("tensor", "dp", None),
        P("tensor", "dp", None),
        P("tensor", "dp", None),
        P(None, "tensor"),
    )
    return jax.shard_map(local, mesh=mesh, in_specs=in_specs, out_specs=out_specs, check_vma=False)
```

```python
import jax
import jax.numpy as jnp
from jax import lax
from jax.experimental import pallas as pl
from jax.experimental.pallas import tpu as pltpu
from jax.sharding import PartitionSpec as P

MESH = pl.DeviceIdType.MESH
F32, BF16 = jnp.float32, jnp.bfloat16
CHUNKS = (1, 2, 2, 2, 2, 2, 2)
DOWN = "BRRABAA"
UP = "ARRRRBA"
FIRST = tuple(sum(CHUNKS[:k]) for k in range(len(CHUNKS)))
TILES = sum(CHUNKS)
ORDER = (
    ("send", 1), ("bsend", 0), ("bsend", 4), ("send", 2), ("send", 3), ("relay", 1), ("bred", 0),
    ("relay", 2), ("send", 5), ("redx", 3), ("redx", 1), ("upd", 0), ("send", 6), ("redx", 2),
    ("bred", 4), ("upd", 3), ("redx", 5), ("upd", 1), ("spread", 0), ("upd", 2), ("redx", 6),
    ("upd", 4), ("upd", 5), ("spread", 3), ("spread", 1), ("upd", 6), ("gath", 0), ("spread", 2),
    ("spread", 4), ("bspread", 5), ("gath", 3), ("serve", 0), ("gath", 1), ("spread", 6),
    ("bgath", 5), ("gath", 2), ("fwd", 3), ("gath", 4), ("fwd", 1), ("fwd", 2), ("gath", 6),
    ("serve", 3), ("fwd", 4), ("serve", 1), ("serve", 2), ("serve", 5), ("serve", 6), ("serve", 4),
)


def kernel(
    g_hbm, m_hbm, f_hbm, s_hbm,
    om, of, os, served,
    gv, mv, fv, sv, perm, parts, got, passed, sums, got_sums, fresh, landed, mine, crossed, wide,
    heard, load_sem, x_send, y_send, z_send, w_send, a_send, x_recv, y_recv, z_recv, w_recv, a_recv, p_recv, f_recv,
):
    k0 = ORDER[0][1]
    lo, hi = FIRST[k0] * 128, (FIRST[k0] + CHUNKS[k0]) * 128
    width = TILES * 128

    def fetch(first, last, sem):
        for i in range(0, 32 * width, width):
            cut = pl.ds(i + first, last - first)
            pltpu.make_async_copy(g_hbm.at[:, cut], gv.at[:, cut], sem).start()

    fetch(lo, hi, load_sem.at[0])
    dp, tn = lax.axis_index("dp"), lax.axis_index("tensor")
    x, yl = dp // 4, dp % 4
    z, yh, core = tn // 4, (tn // 2) % 2, tn % 2
    y = yh * 4 + yl
    q = core * 8 + z
    right, left, across = (x + 1) % 4, (x + 3) % 4, (x + 2) % 4

    def device(dx=0, dy=0, dz=0, dc=0):
        to_y = (y + dy) % 8
        return ((x + dx) % 4) * 4 + to_y % 4, ((z + dz) % 8) * 4 + (to_y // 4) * 2 + (core + dc) % 2

    to_right, to_left = device(dx=1), device(dx=3)
    x_peers = [((x + d) % 4, device(dx=d)) for d in (2, 1, 3)]
    lo_peers = [((yl + d) % 4, (x * 4 + (yl + d) % 4, tn)) for d in range(1, 4)]
    y_peers = [(((y + d) % 8) // 4, device(dy=d)) for d in (4, 3, 5, 2, 6, 1, 7)]
    z_peers = [
        (((core + dc) % 2) * 8 + (z + dz) % 8, device(dz=dz, dc=dc))
        for dz in (4, 3, 5, 2, 6, 1, 7, 0) for dc in (1, 0) if (dz, dc) != (0, 0)
    ]

    barrier = pltpu.get_barrier_semaphore()
    steps = (1, 7)
    greeted = [peer for _, peer in x_peers + lo_peers]
    greeted += [device(dy=d) for d in steps] + [device(dc=1)]
    greeted += [device(dz=d, dc=dc) for d in steps for dc in range(2)]
    for peer in greeted:
        pl.semaphore_signal(barrier, inc=1, device_id=peer, device_id_type=MESH)

    def hail(turn):
        for d in ((1, 7), (2, 6))[turn]:
            pl.semaphore_signal(heard.at[turn, 0], inc=1, device_id=device(dy=d), device_id_type=MESH)
            pl.semaphore_signal(heard.at[turn, 1], inc=1, device_id=device(dz=d), device_id_type=MESH)

    def hear(turn):
        for way in range(2):
            pl.semaphore_wait(heard.at[turn, way], 2)

    row = lax.broadcasted_iota(jnp.int32, (256, 256), 0)
    col = lax.broadcasted_iota(jnp.int32, (256, 256), 1)
    perm[...] = jnp.where(col == (row % 16) * 16 + row // 16, 1.0, 0.0).astype(BF16)

    if lo:
        fetch(0, lo, load_sem.at[4])
    fetch(hi, width, load_sem.at[4])
    loads = [
        pltpu.make_async_copy(src, dst, load_sem.at[1 + i])
        for i, (src, dst) in enumerate(((m_hbm, mv), (f_hbm, fv), (s_hbm, sv)))
    ]
    for copy in loads:
        copy.start()

    def swap(rows):
        return jnp.dot(perm[...], rows, preferred_element_type=F32).astype(BF16)

    def wait(tiles, sem):
        ref = gv.at[:, 0 : tiles * 128]
        pltpu.make_async_copy(ref, ref, sem).wait()

    def remote(src, dst, send, recv, peer):
        pltpu.make_async_remote_copy(
            src_ref=src, dst_ref=dst, send_sem=send, recv_sem=recv, device_id=peer, device_id_type=MESH
        ).start()

    def tiles(k):
        return range(FIRST[k], FIRST[k] + CHUNKS[k])

    def span(k, per):
        return pl.ds(FIRST[k] * per, CHUNKS[k] * per)

    def split(k):
        for c in tiles(k):
            halves = []
            for h in range(2):
                columns = [((i % 8 * 4 + h * 2 + i // 8) * TILES + c) * 128 for i in range(16)]
                halves.append(jnp.concatenate([gv[:, at : at + 128] for at in columns], axis=0))
            out = swap(jnp.concatenate(halves, axis=1))
            for j in range(16):
                for h in range(2):
                    parts[j // 4, j % 4, c * 32 + h * 16 : c * 32 + h * 16 + 16, :] = (
                        out[j * 16 : j * 16 + 16, h * 128 : h * 128 + 128]
                    )

    def send(k):
        split(k)
        if (send.__name__, k) == ORDER[0]:
            pl.semaphore_wait(barrier, len(greeted))
        at = span(k, 32)
        if DOWN[k] == "R":
            remote(parts.at[across, 0:2, at], passed.at[0, :, at], x_send, p_recv.at[k], to_right)
            remote(parts.at[across, 2:4, at], passed.at[1, :, at], x_send, p_recv.at[k], to_left)
            remote(parts.at[right, 2:4, at], got.at[0, 2:4, at], x_send, x_recv.at[k], to_right)
            remote(parts.at[left, 0:2, at], got.at[1, 0:2, at], x_send, x_recv.at[k], to_left)
        else:
            for d, (to, peer) in enumerate(x_peers):
                remote(parts.at[to, :, at], got.at[d, :, at], x_send, x_recv.at[k], peer)

    def relay(k):
        wait(CHUNKS[k] * 8, p_recv.at[k])
        at = span(k, 32)
        for way, (to, first, peer) in enumerate(((right, 0, to_right), (left, 2, to_left))):
            for i in range(2):
                passed[way, i, at, :] = (
                    passed[way, i, at, :].astype(F32) + parts[to, first + i, at, :].astype(F32)
                ).astype(BF16)
            remote(passed.at[way, :, at], got.at[way, first : first + 2, at], x_send, x_recv.at[k], peer)

    def received(k):
        return 2 if DOWN[k] == "R" else 3

    def redx(k):
        wait(CHUNKS[k] * 8 * received(k), x_recv.at[k])
        at = span(k, 32)
        for d, (to, peer) in enumerate(lo_peers):
            total = parts[x, to, at, :].astype(F32)
            for i in range(received(k)):
                total += got[i, to, at, :].astype(F32)
            sums[d, at, :] = total.astype(BF16)
            remote(sums.at[d, at], got_sums.at[d, at], y_send, y_recv.at[k], peer)

    def bsend(k):
        split(k)
        at = span(k, 32)
        for d, (to, peer) in enumerate(lo_peers):
            remote(parts.at[:, to, at], got.at[d, :, at], x_send, x_recv.at[k], peer)

    def bred(k):
        wait(CHUNKS[k] * 24, x_recv.at[k])
        at = span(k, 32)
        for d, (to, peer) in enumerate(x_peers):
            total = parts[to, yl, at, :].astype(F32)
            for i in range(3):
                total += got[i, to, at, :].astype(F32)
            sums[d, at, :] = total.astype(BF16)
            remote(sums.at[d, at], got_sums.at[d, at], y_send, y_recv.at[k], peer)

    def upd(k):
        wait(CHUNKS[k] * 6, y_recv.at[k])
        own = x if DOWN[k] == "B" else yl
        for c in tiles(k):
            for h in range(2):
                rows = pl.ds(c * 32 + h * 16, 16)
                total = parts[x, yl, rows, :].astype(F32)
                for i in range(received(k)):
                    total += got[i, own, rows, :].astype(F32)
                for i in range(3):
                    total += got_sums[i, rows, :].astype(F32)
                total = total / 16
                for e in range(2):
                    gradient = total[e * 8 : e * 8 + 8]
                    at = pl.ds(h * 2 * TILES + e * TILES + c, 8, stride=4 * TILES)
                    first = 0.9 * fv[at, :] + 0.1 * gradient
                    second = 0.95 * sv[at, :] + 0.05 * gradient * gradient
                    of[at, :] = first
                    os[at, :] = second
                    step = first / (1.0 - 0.9**10) / (jnp.sqrt(second / (1.0 - 0.95**10)) + 1e-08)
                    old = mv[at, :]
                    new = old - 0.5 * (step + 0.1 * old)
                    om[at, :] = new
                    for i in range(8):
                        fresh[c, h, e * 8 + i, :, :] = new[i : i + 1]
        at = span(k, 1)
        for to, peer in z_peers:
            remote(fresh.at[at, :, to], landed.at[at, :, q], z_send, z_recv.at[k], peer)
        pltpu.make_async_copy(fresh.at[at, :, q], landed.at[at, :, q], z_recv.at[k]).start()

    def collect(k):
        wait(CHUNKS[k] * 4, z_recv.at[k])
        for c in tiles(k):
            for h in range(2):
                block = jnp.concatenate([landed[c, h, i, :, :] for i in range(16)], axis=0)
                mine[h, c * 16 : c * 16 + 16, :] = block.astype(BF16)

    def spread(k):
        collect(k)
        at = span(k, 16)
        for to, peer in y_peers:
            remote(mine.at[to, at], wide.at[x, yl, yh, at], w_send, w_recv.at[k], peer)
        pltpu.make_async_copy(mine.at[yh, at], wide.at[x, yl, yh, at], w_recv.at[k]).start()

    def gath(k):
        wait(CHUNKS[k] * 8, w_recv.at[k])
        own = wide.at[x, :, :, span(k, 16)]
        for peer in (to_right, to_left) if UP[k] == "R" else [peer for _, peer in x_peers]:
            remote(own, own, a_send, a_recv.at[k], peer)

    def fwd(k):
        wait(CHUNKS[k] * 16, a_recv.at[k])
        for source, first, peer in ((left, 0, to_right), (right, 2, to_left)):
            block = wide.at[source, first : first + 2, :, span(k, 16)]
            remote(block, block, a_send, f_recv.at[k], peer)

    def bspread(k):
        collect(k)
        at = span(k, 16)
        for _, peer in x_peers:
            remote(mine.at[:, at], crossed.at[x, :, at], w_send, w_recv.at[k], peer)
        pltpu.make_async_copy(mine.at[:, at], crossed.at[x, :, at], w_recv.at[k]).start()

    def bgath(k):
        wait(CHUNKS[k] * 8, w_recv.at[k])
        at = span(k, 16)
        for to, peer in y_peers:
            remote(crossed.at[:, to, at], wide.at[:, yl, yh, at], a_send, a_recv.at[k], peer)
        pltpu.make_async_copy(crossed.at[:, yh, at], wide.at[:, yl, yh, at], a_recv.at[k]).start()

    def serve(k):
        if UP[k] == "R":
            wait(CHUNKS[k] * 8, f_recv.at[k])
        else:
            wait(CHUNKS[k] * (32 if UP[k] == "B" else 24), a_recv.at[k])
        for c in tiles(k):
            halves = [
                jnp.concatenate([wide[j // 4, j % 4, h, c * 16 : c * 16 + 16, :] for j in range(16)], axis=0)
                for h in range(2)
            ]
            out = swap(jnp.concatenate(halves, axis=1))
            for i in range(16):
                for h in range(2):
                    t = i % 8 * 4 + h * 2 + i // 8
                    served[t * 16 : t * 16 + 16, c * 128 : c * 128 + 128] = (
                        out[i * 16 : i * 16 + 16, h * 128 : h * 128 + 128]
                    )

    stages = {
        f.__name__: f for f in (send, relay, redx, bsend, bred, upd, spread, gath, fwd, bspread, bgath, serve)
    }
    wait(CHUNKS[k0] * 32, load_sem.at[0])
    hailed = [name in ("send", "bsend") for name, _ in ORDER].index(False)
    for i, (stage, k) in enumerate(ORDER):
        if i == 1:
            hail(0)
            wait((TILES - CHUNKS[k0]) * 32, load_sem.at[4])
        before = [name for name, _ in ORDER[:i]]
        if i == hailed:
            hear(0)
            hail(1)
        if stage == "upd" and "upd" not in before:
            hear(1)
            for copy in loads:
                copy.wait()
        stages[stage](k)

    crosswise = sum(c for c, kind in zip(CHUNKS, UP) if kind == "B")
    straight = TILES - crosswise
    wait(TILES * 24, x_send)
    wait(TILES * 6, y_send)
    sent = landed.at[:, :, 0:15]
    pltpu.make_async_copy(sent, sent, z_send).wait()
    wait(straight * 7 + crosswise * 6, w_send)
    wait(straight * 24 + crosswise * 28, a_send)


def store(*refs):
    copies = [pltpu.make_async_copy(refs[i], refs[4 + i], refs[8].at[i]) for i in (3, 0, 1, 2)]
    for copy in copies:
        copy.start()
    for copy in copies:
        copy.wait()


def local(grads, master, first_moment, second_moment):
    n = len(CHUNKS)
    rows = TILES * 32
    dma = pltpu.SemaphoreType.DMA
    vmem = pltpu.VMEM
    shapes = ((rows, 128), F32), ((rows, 128), F32), ((rows, 128), F32), ((512, TILES * 128), BF16)
    outs = pl.pallas_call(
        kernel,
        name="refit",
        out_shape=[vmem(*shape) for shape in shapes],
        in_specs=[pl.BlockSpec(memory_space=pltpu.HBM)] * 4,
        out_specs=[pl.BlockSpec(memory_space=vmem)] * 4,
        scratch_shapes=[
            vmem((16, rows * 128), BF16),
            vmem((rows, 128), F32),
            vmem((rows, 128), F32),
            vmem((rows, 128), F32),
            vmem((256, 256), BF16),
            vmem((4, 4, rows, 128), BF16),
            vmem((3, 4, rows, 128), BF16),
            vmem((2, 2, rows, 128), BF16),
            vmem((3, rows, 128), BF16),
            vmem((3, rows, 128), BF16),
            vmem((TILES, 2, 16, 1, 128), F32),
            vmem((TILES, 2, 16, 1, 128), F32),
            vmem((2, TILES * 16, 128), BF16),
            vmem((4, 2, TILES * 16, 128), BF16),
            vmem((4, 4, 2, TILES * 16, 128), BF16),
            pltpu.SemaphoreType.REGULAR((2, 2)),
            dma((5,)),
            *([dma] * 5),
            *([dma((n,))] * 7),
        ],
        compiler_params=pltpu.CompilerParams(
            collective_id=0, has_side_effects=True, vmem_limit_bytes=60 * 2**20
        ),
    )(
        *(
            pltpu.with_memory_space_constraint(v, pltpu.HBM)
            for v in (
                grads.reshape(16, rows * 128),
                master.reshape(rows, 128),
                first_moment.reshape(rows, 128),
                second_moment.reshape(rows, 128),
            )
        )
    )
    outs = pl.pallas_call(
        store,
        name="store",
        out_shape=[jax.ShapeDtypeStruct(*shape) for shape in shapes],
        in_specs=[pl.BlockSpec(memory_space=vmem)] * 4,
        out_specs=[pl.BlockSpec(memory_space=pltpu.HBM)] * 4,
        scratch_shapes=[dma((4,))],
        compiler_params=pltpu.CompilerParams(vmem_limit_bytes=2**20),
    )(*outs)
    new_master, new_first, new_second, served = outs
    shape = master.shape
    return new_master.reshape(shape), new_first.reshape(shape), new_second.reshape(shape), served


def solution(mesh):
    in_specs = (
        P("dp", "tensor", None, None),
        P("tensor", "dp", None),
        P("tensor", "dp", None),
        P("tensor", "dp", None),
    )
    out_specs = (
        P("tensor", "dp", None),
        P("tensor", "dp", None),
        P("tensor", "dp", None),
        P(None, "tensor"),
    )
    return jax.shard_map(local, mesh=mesh, in_specs=in_specs, out_specs=out_specs, check_vma=False)
```

```python
import jax
import jax.numpy as jnp
from jax import lax
from jax.experimental import pallas as pl
from jax.experimental.pallas import tpu as pltpu
from jax.sharding import PartitionSpec as P

MESH = pl.DeviceIdType.MESH
F32, BF16 = jnp.float32, jnp.bfloat16
CHUNKS = (1, 2, 2, 2, 2, 2, 2)
DOWN = "BRRABAA"
UP = "ARRRRBA"
FIRST = tuple(sum(CHUNKS[:k]) for k in range(len(CHUNKS)))
TILES = sum(CHUNKS)
PASSED = [k for k, way in enumerate(DOWN) if way == "R"]
FORWARDED = [k for k, way in enumerate(UP) if way == "R"]
ORDER = (
    ("send", 1), ("bsend", 0), ("bsend", 4), ("send", 2), ("send", 3), ("relay", 1), ("bred", 0),
    ("relay", 2), ("send", 5), ("redx", 3), ("redx", 1), ("upd", 0), ("send", 6), ("redx", 2),
    ("bred", 4), ("upd", 3), ("redx", 5), ("upd", 1), ("spread", 0), ("upd", 2), ("redx", 6),
    ("upd", 4), ("upd", 5), ("spread", 3), ("spread", 1), ("upd", 6), ("gath", 0), ("spread", 2),
    ("spread", 4), ("bspread", 5), ("gath", 3), ("serve", 0), ("gath", 1), ("spread", 6),
    ("bgath", 5), ("gath", 2), ("fwd", 3), ("gath", 4), ("fwd", 1), ("fwd", 2), ("gath", 6),
    ("serve", 3), ("fwd", 4), ("serve", 1), ("serve", 2), ("serve", 5), ("serve", 6), ("serve", 4),
)


def kernel(
    g_hbm, m_hbm, f_hbm, s_hbm,
    om, of, os, served,
    gv, mv, fv, sv, perm, parts, got, passed, sums, got_sums, fresh, landed, mine, crossed, wide,
    heard, load_sem, x_send, y_send, z_send, w_send, a_send, x_recv, y_recv, z_recv, w_recv, a_recv, p_recv, f_recv,
):
    dp, tn = lax.axis_index("dp"), lax.axis_index("tensor")
    x, yl = dp // 4, dp % 4
    z, yh, core = tn // 4, (tn // 2) % 2, tn % 2
    y = yh * 4 + yl
    q = core * 8 + z
    right, left, across = (x + 1) % 4, (x + 3) % 4, (x + 2) % 4

    def device(dx=0, dy=0, dz=0, dc=0):
        to_y = (y + dy) % 8
        return ((x + dx) % 4) * 4 + to_y % 4, ((z + dz) % 8) * 4 + (to_y // 4) * 2 + (core + dc) % 2

    to_right, to_left = device(dx=1), device(dx=3)
    x_peers = [((x + d) % 4, device(dx=d)) for d in (2, 1, 3)]
    lo_peers = [((yl + d) % 4, (x * 4 + (yl + d) % 4, tn)) for d in range(1, 4)]
    y_peers = [(((y + d) % 8) // 4, device(dy=d)) for d in (4, 3, 5, 2, 6, 1, 7)]
    z_peers = [
        (((core + dc) % 2) * 8 + (z + dz) % 8, device(dz=dz, dc=dc))
        for dz in (4, 3, 5, 2, 6, 1, 7, 0) for dc in (1, 0) if (dz, dc) != (0, 0)
    ]

    barrier = pltpu.get_barrier_semaphore()
    steps = (1, 7)
    greeted = [peer for _, peer in x_peers + lo_peers]
    greeted += [device(dy=d) for d in steps] + [device(dc=1)]
    greeted += [device(dz=d, dc=dc) for d in steps for dc in range(2)]
    for peer in greeted:
        pl.semaphore_signal(barrier, inc=1, device_id=peer, device_id_type=MESH)

    k0 = ORDER[0][1]
    lo, hi = FIRST[k0] * 128, (FIRST[k0] + CHUNKS[k0]) * 128
    width = TILES * 128

    def fetch(first, last, sem):
        for i in range(0, 32 * width, width):
            cut = pl.ds(i + first, last - first)
            pltpu.make_async_copy(g_hbm.at[:, cut], gv.at[:, cut], sem).start()

    fetch(lo, hi, load_sem.at[0])
    def hail(turn):
        for d in ((1, 7), (2, 6))[turn]:
            pl.semaphore_signal(heard.at[turn, 0], inc=1, device_id=device(dy=d), device_id_type=MESH)
            pl.semaphore_signal(heard.at[turn, 1], inc=1, device_id=device(dz=d), device_id_type=MESH)

    def hear(turn):
        for way in range(2):
            pl.semaphore_wait(heard.at[turn, way], 2)

    row = lax.broadcasted_iota(jnp.int32, (256, 256), 0)
    col = lax.broadcasted_iota(jnp.int32, (256, 256), 1)
    perm[...] = jnp.where(col == (row % 16) * 16 + row // 16, 1.0, 0.0).astype(BF16)

    if lo:
        fetch(0, lo, load_sem.at[4])
    fetch(hi, width, load_sem.at[4])
    loads = [
        pltpu.make_async_copy(src, dst, load_sem.at[1 + i])
        for i, (src, dst) in enumerate(((m_hbm, mv), (f_hbm, fv), (s_hbm, sv)))
    ]
    for copy in loads:
        copy.start()

    def swap(rows):
        return jnp.dot(perm[...], rows, preferred_element_type=F32).astype(BF16)

    def wait(tiles, sem):
        ref = gv.at[:, 0 : tiles * 128]
        pltpu.make_async_copy(ref, ref, sem).wait()

    def remote(src, dst, send, recv, peer):
        pltpu.make_async_remote_copy(
            src_ref=src, dst_ref=dst, send_sem=send, recv_sem=recv, device_id=peer, device_id_type=MESH
        ).start()

    def tiles(k):
        return range(FIRST[k], FIRST[k] + CHUNKS[k])

    def span(k, per):
        return pl.ds(FIRST[k] * per, CHUNKS[k] * per)

    def split(k):
        for c in tiles(k):
            halves = []
            for h in range(2):
                columns = [((i % 8 * 4 + h * 2 + i // 8) * TILES + c) * 128 for i in range(16)]
                halves.append(jnp.concatenate([gv[:, at : at + 128] for at in columns], axis=0))
            out = swap(jnp.concatenate(halves, axis=1))
            for j in range(16):
                for h in range(2):
                    parts[j // 4, j % 4, c * 32 + h * 16 : c * 32 + h * 16 + 16, :] = (
                        out[j * 16 : j * 16 + 16, h * 128 : h * 128 + 128]
                    )

    def enter(k):
        if k == ORDER[0][1]:
            pl.semaphore_wait(barrier, len(greeted))

    def send(k):
        split(k)
        enter(k)
        at = span(k, 32)
        if DOWN[k] == "R":
            remote(parts.at[across, 0:2, at], passed.at[0, :, at], x_send, p_recv.at[PASSED.index(k)], to_right)
            remote(parts.at[across, 2:4, at], passed.at[1, :, at], x_send, p_recv.at[PASSED.index(k)], to_left)
            remote(parts.at[right, 2:4, at], got.at[0, 2:4, at], x_send, x_recv.at[k], to_right)
            remote(parts.at[left, 0:2, at], got.at[1, 0:2, at], x_send, x_recv.at[k], to_left)
        else:
            for d, (to, peer) in enumerate(x_peers):
                remote(parts.at[to, :, at], got.at[d, :, at], x_send, x_recv.at[k], peer)

    def relay(k):
        wait(CHUNKS[k] * 8, p_recv.at[PASSED.index(k)])
        at = span(k, 32)
        for way, (to, first, peer) in enumerate(((right, 0, to_right), (left, 2, to_left))):
            for i in range(2):
                passed[way, i, at, :] = (
                    passed[way, i, at, :].astype(F32) + parts[to, first + i, at, :].astype(F32)
                ).astype(BF16)
            remote(passed.at[way, :, at], got.at[way, first : first + 2, at], x_send, x_recv.at[k], peer)

    def received(k):
        return 2 if DOWN[k] == "R" else 3

    def redx(k):
        wait(CHUNKS[k] * 8 * received(k), x_recv.at[k])
        at = span(k, 32)
        for d, (to, peer) in enumerate(lo_peers):
            total = parts[x, to, at, :].astype(F32)
            for i in range(received(k)):
                total += got[i, to, at, :].astype(F32)
            sums[d, at, :] = total.astype(BF16)
            remote(sums.at[d, at], got_sums.at[d, at], y_send, y_recv.at[k], peer)

    def bsend(k):
        split(k)
        enter(k)
        at = span(k, 32)
        for d, (to, peer) in enumerate(lo_peers):
            remote(parts.at[:, to, at], got.at[d, :, at], x_send, x_recv.at[k], peer)

    def bred(k):
        wait(CHUNKS[k] * 24, x_recv.at[k])
        at = span(k, 32)
        for d, (to, peer) in enumerate(x_peers):
            total = parts[to, yl, at, :].astype(F32)
            for i in range(3):
                total += got[i, to, at, :].astype(F32)
            sums[d, at, :] = total.astype(BF16)
            remote(sums.at[d, at], got_sums.at[d, at], y_send, y_recv.at[k], peer)

    def upd(k):
        wait(CHUNKS[k] * 6, y_recv.at[k])
        own = x if DOWN[k] == "B" else yl
        for c in tiles(k):
            for h in range(2):
                rows = pl.ds(c * 32 + h * 16, 16)
                total = parts[x, yl, rows, :].astype(F32)
                for i in range(received(k)):
                    total += got[i, own, rows, :].astype(F32)
                for i in range(3):
                    total += got_sums[i, rows, :].astype(F32)
                total = total / 16
                for e in range(2):
                    gradient = total[e * 8 : e * 8 + 8]
                    at = pl.ds(h * 2 * TILES + e * TILES + c, 8, stride=4 * TILES)
                    first = 0.9 * fv[at, :] + 0.1 * gradient
                    second = 0.95 * sv[at, :] + 0.05 * gradient * gradient
                    of[at, :] = first
                    os[at, :] = second
                    step = first / (1.0 - 0.9**10) / (jnp.sqrt(second / (1.0 - 0.95**10)) + 1e-08)
                    old = mv[at, :]
                    new = old - 0.5 * (step + 0.1 * old)
                    om[at, :] = new
                    for i in range(8):
                        fresh[c, h, e * 8 + i, :, :] = new[i : i + 1]
        at = span(k, 1)
        for to, peer in z_peers:
            remote(fresh.at[at, :, to], landed.at[at, :, q], z_send, z_recv.at[k], peer)
        pltpu.make_async_copy(fresh.at[at, :, q], landed.at[at, :, q], z_recv.at[k]).start()

    def collect(k):
        wait(CHUNKS[k] * 4, z_recv.at[k])
        for c in tiles(k):
            for h in range(2):
                block = jnp.concatenate([landed[c, h, i, :, :] for i in range(16)], axis=0)
                mine[h, c * 16 : c * 16 + 16, :] = block.astype(BF16)

    def spread(k):
        collect(k)
        at = span(k, 16)
        for to, peer in y_peers:
            remote(mine.at[to, at], wide.at[x, yl, yh, at], w_send, w_recv.at[k], peer)
        pltpu.make_async_copy(mine.at[yh, at], wide.at[x, yl, yh, at], w_recv.at[k]).start()

    def gath(k):
        wait(CHUNKS[k] * 8, w_recv.at[k])
        own = wide.at[x, :, :, span(k, 16)]
        for peer in (to_right, to_left) if UP[k] == "R" else [peer for _, peer in x_peers]:
            remote(own, own, a_send, a_recv.at[k], peer)

    def fwd(k):
        wait(CHUNKS[k] * 16, a_recv.at[k])
        for source, first, peer in ((left, 0, to_right), (right, 2, to_left)):
            block = wide.at[source, first : first + 2, :, span(k, 16)]
            remote(block, block, a_send, f_recv.at[FORWARDED.index(k)], peer)

    def bspread(k):
        collect(k)
        at = span(k, 16)
        for _, peer in x_peers:
            remote(mine.at[:, at], crossed.at[x, :, at], w_send, w_recv.at[k], peer)
        pltpu.make_async_copy(mine.at[:, at], crossed.at[x, :, at], w_recv.at[k]).start()

    def bgath(k):
        wait(CHUNKS[k] * 8, w_recv.at[k])
        at = span(k, 16)
        for to, peer in y_peers:
            remote(crossed.at[:, to, at], wide.at[:, yl, yh, at], a_send, a_recv.at[k], peer)
        pltpu.make_async_copy(crossed.at[:, yh, at], wide.at[:, yl, yh, at], a_recv.at[k]).start()

    def serve(k):
        if UP[k] == "R":
            wait(CHUNKS[k] * 8, f_recv.at[FORWARDED.index(k)])
        else:
            wait(CHUNKS[k] * (32 if UP[k] == "B" else 24), a_recv.at[k])
        for c in tiles(k):
            halves = [
                jnp.concatenate([wide[j // 4, j % 4, h, c * 16 : c * 16 + 16, :] for j in range(16)], axis=0)
                for h in range(2)
            ]
            out = swap(jnp.concatenate(halves, axis=1))
            for i in range(16):
                for h in range(2):
                    t = i % 8 * 4 + h * 2 + i // 8
                    served[t * 16 : t * 16 + 16, c * 128 : c * 128 + 128] = (
                        out[i * 16 : i * 16 + 16, h * 128 : h * 128 + 128]
                    )

    stages = {
        f.__name__: f for f in (send, relay, redx, bsend, bred, upd, spread, gath, fwd, bspread, bgath, serve)
    }
    wait(CHUNKS[k0] * 32, load_sem.at[0])
    hailed = [name in ("send", "bsend") for name, _ in ORDER].index(False)
    for i, (stage, k) in enumerate(ORDER):
        if i == 1:
            hail(0)
            wait((TILES - CHUNKS[k0]) * 32, load_sem.at[4])
        before = [name for name, _ in ORDER[:i]]
        if i == hailed:
            hear(0)
            hail(1)
        if stage == "upd" and "upd" not in before:
            hear(1)
            for copy in loads:
                copy.wait()
        stages[stage](k)

    crosswise = sum(c for c, kind in zip(CHUNKS, UP) if kind == "B")
    straight = TILES - crosswise
    wait(TILES * 24, x_send)
    wait(TILES * 6, y_send)
    sent = landed.at[:, :, 0:15]
    pltpu.make_async_copy(sent, sent, z_send).wait()
    wait(straight * 7 + crosswise * 6, w_send)
    wait(straight * 24 + crosswise * 28, a_send)


def store(*refs):
    copies = [pltpu.make_async_copy(refs[i], refs[4 + i], refs[8].at[i]) for i in (3, 0, 1, 2)]
    for copy in copies:
        copy.start()
    for copy in copies:
        copy.wait()


def local(grads, master, first_moment, second_moment):
    n = len(CHUNKS)
    rows = TILES * 32
    dma = pltpu.SemaphoreType.DMA
    vmem = pltpu.VMEM
    shapes = ((rows, 128), F32), ((rows, 128), F32), ((rows, 128), F32), ((512, TILES * 128), BF16)
    outs = pl.pallas_call(
        kernel,
        name="refit",
        out_shape=[vmem(*shape) for shape in shapes],
        in_specs=[pl.BlockSpec(memory_space=pltpu.HBM)] * 4,
        out_specs=[pl.BlockSpec(memory_space=vmem)] * 4,
        scratch_shapes=[
            vmem((16, rows * 128), BF16),
            vmem((rows, 128), F32),
            vmem((rows, 128), F32),
            vmem((rows, 128), F32),
            vmem((256, 256), BF16),
            vmem((4, 4, rows, 128), BF16),
            vmem((3, 4, rows, 128), BF16),
            vmem((2, 2, rows, 128), BF16),
            vmem((3, rows, 128), BF16),
            vmem((3, rows, 128), BF16),
            vmem((TILES, 2, 16, 1, 128), F32),
            vmem((TILES, 2, 16, 1, 128), F32),
            vmem((2, TILES * 16, 128), BF16),
            vmem((4, 2, TILES * 16, 128), BF16),
            vmem((4, 4, 2, TILES * 16, 128), BF16),
            pltpu.SemaphoreType.REGULAR((2, 2)),
            dma((5,)),
            *([dma] * 5),
            *([dma((n,))] * 5),
            dma((max(1, len(PASSED)),)), dma((max(1, len(FORWARDED)),)),
        ],
        compiler_params=pltpu.CompilerParams(
            collective_id=0, has_side_effects=True, vmem_limit_bytes=60 * 2**20
        ),
    )(
        *(
            pltpu.with_memory_space_constraint(v, pltpu.HBM)
            for v in (
                grads.reshape(16, rows * 128),
                master.reshape(rows, 128),
                first_moment.reshape(rows, 128),
                second_moment.reshape(rows, 128),
            )
        )
    )
    outs = pl.pallas_call(
        store,
        name="store",
        out_shape=[jax.ShapeDtypeStruct(*shape) for shape in shapes],
        in_specs=[pl.BlockSpec(memory_space=vmem)] * 4,
        out_specs=[pl.BlockSpec(memory_space=pltpu.HBM)] * 4,
        scratch_shapes=[dma((4,))],
        compiler_params=pltpu.CompilerParams(vmem_limit_bytes=2**20),
    )(*outs)
    new_master, new_first, new_second, served = outs
    shape = master.shape
    return new_master.reshape(shape), new_first.reshape(shape), new_second.reshape(shape), served


def solution(mesh):
    in_specs = (
        P("dp", "tensor", None, None),
        P("tensor", "dp", None),
        P("tensor", "dp", None),
        P("tensor", "dp", None),
    )
    out_specs = (
        P("tensor", "dp", None),
        P("tensor", "dp", None),
        P("tensor", "dp", None),
        P(None, "tensor"),
    )
    return jax.shard_map(local, mesh=mesh, in_specs=in_specs, out_specs=out_specs, check_vma=False)
```
